512 devices in a mesh: blk: 64 (over y_lo, z, x), rep: 8 (over y_hi, core).
Axes of the slice: x: 4, y: 8 (y_hi: 4, y_lo: 2; y = y_hi * 2 + y_lo), z: 8, core: 2. Of those that a mesh axis runs over, the one named last changes fastest.
Arguments:
- features: bfloat16 [524288, 256], P(('blk', 'rep')), may hold values from -6 to 6
- block_cols: int32 [4096, 44], P(('blk', 'rep')), may hold values from 0 to 4095, as said below
- adjacency: int32 [4096, 44, 4, 128], P(('blk', 'rep')), may hold values from 0 to 511, as said below
- w_self: bfloat16 [256, 256], replicated, may hold values from -0.375 to 0.375
- w_neigh: bfloat16 [256, 256], replicated, may hold values from -0.375 to 0.375
- bias: float32 [256], replicated, may hold values from -4 to 4
Outputs:
- mixed: bfloat16 [524288, 256], P(('blk', 'rep'))
The draws below stay inside these ranges and needn't reach their ends.
Inputs may be any that keep to these rules, and one draw needn't show every extreme that they name: `block_cols`: the 44 numbers of a block row b are different, and each lies in the group of block b or in the group just before or after it on a closed loop of groups, group of block c being c // 64. `adjacency`: each entry is 4 times a column within the block plus an edge count of 0 to 3.
All inputs are finite; a program needn't handle non-finite values.
Results may differ from the reference program's by a relative error of at most 0.0021.
Values may be sent and summed in bfloat16 or wider, within the bound.
No kernel may reach another device: no remote copies, remote signals or barrier semaphores. Data moves between devices by JAX's collectives and lax.ppermute only.
A program may use at most 128 MiB of HBM per device.

```python
import jax
import jax.numpy as jnp
from jax import lax

F = 256
H = 256
BS = 128
EDGE = 4
GROUP_BLOCKS = 64
NNZB = 44
NODES = 524288


def draw_block_cols(key, part):
    key = jax.random.fold_in(key, 1)
    rows = NODES // BS
    groups = NODES // (BS * GROUP_BLOCKS)
    keys = jax.random.split(key, rows)
    picks = jax.vmap(lambda k: jax.random.permutation(k, 3 * GROUP_BLOCKS)[:NNZB])(keys).astype(jnp.int32)
    own_group = jnp.arange(rows, dtype=jnp.int32)[:, None] // GROUP_BLOCKS
    shift = picks // GROUP_BLOCKS - 1
    target = (own_group + shift + groups) % groups
    return (target * GROUP_BLOCKS + picks % GROUP_BLOCKS).astype(jnp.int32)


def draw_adjacency(key, part):
    key = jax.random.fold_in(key, 2)
    k_col, k_val, k_live = jax.random.split(key, 3)
    shape = (NODES // BS, NNZB, EDGE, BS)
    column = jax.random.randint(k_col, shape, 0, BS)
    value = jax.random.randint(k_val, shape, 0, 4)
    live = (jax.random.randint(k_live, (NODES // BS, 1, 1, BS), 0, 16) != 0).astype(jnp.int32)
    return (4 * column + value * live).astype(jnp.int32)


def steps_of(own_key, extent, shards, low, largest):
    def one(axis_at, shards_of):
        steps = jax.random.uniform(jax.random.fold_in(jax.random.fold_in(own_key, 6), axis_at), (shards_of,), jnp.float32, low / len(shards), largest / len(shards))
        return jnp.repeat(jnp.exp(steps), extent[axis_at] // shards_of).reshape((-1,) + (1,) * (len(extent) - axis_at - 1))

    factor_of = one(*shards[0])
    for cut in shards[1:]:
        factor_of = factor_of * one(*cut)
    return factor_of


def centred(own_key, shape, scale, most, shards=(), kind=jnp.bfloat16):
    result = scale * jax.random.normal(own_key, shape, jnp.float32)
    if shards:
        result = result * steps_of(own_key, shape, shards, -0.22, 0.18)
    return jnp.clip(result, -most, most).astype(kind)


def setup_inputs(seed: int = 0) -> dict:
    key_of = jax.random.split(jax.random.key(seed), 7)
    features = centred(key_of[0], (NODES, F), 1.0, 6.0, ((0, 512),))
    block_cols = draw_block_cols(jax.random.fold_in(key_of[6], 71), 0)
    adjacency = draw_adjacency(jax.random.fold_in(key_of[6], 71), 0)
    w_self = centred(key_of[3], (F, H), F ** -0.5, 0.375)
    w_neigh = centred(key_of[4], (F, H), F ** -0.5, 0.375)
    bias = centred(key_of[5], (H,), 1.0, 4.0, (), jnp.float32)
    return {"features": features, "block_cols": block_cols, "adjacency": adjacency, "w_self": w_self, "w_neigh": w_neigh, "bias": bias}


def unpack_counts(words):
    columns = jnp.right_shift(words, 2)
    values = jnp.bitwise_and(words, 3)
    slots, edges, rows = words.shape
    places = jnp.arange(rows, dtype=jnp.int32)
    counts = jnp.zeros((slots, rows, rows), jnp.int32)
    for edge in range(edges):
        match = columns[:, edge, :, None] == places[None, None, :]
        counts = counts + jnp.where(match, values[:, edge, :, None], 0)
    counts = jnp.transpose(counts, (1, 0, 2)).reshape(rows, slots * rows)
    return counts


def reference(features, block_cols, adjacency, w_self, w_neigh, bias):
    width = features.shape[1]
    blocks = features.reshape(NODES // BS, BS, width)

    def one_row(pair):
        cols, words = pair
        counts = unpack_counts(words)
        gathered = jnp.take(blocks, cols.astype(jnp.int32), axis=0).reshape(-1, width)
        summed = jnp.dot(counts.astype(jnp.bfloat16), gathered, preferred_element_type=jnp.float32)
        degree = jnp.sum(counts.astype(jnp.float32), axis=1)
        return summed, degree

    summed, degree = lax.map(one_row, (block_cols, adjacency))
    summed = summed.reshape(NODES, width)
    degree = degree.reshape(NODES, 1)
    neighbour_mean = (summed / jnp.maximum(degree, jnp.float32(1.0))).astype(jnp.bfloat16)
    total = jnp.dot(features, w_self, preferred_element_type=jnp.float32)
    total = total + jnp.dot(neighbour_mean, w_neigh, preferred_element_type=jnp.float32) + bias
    return jnp.maximum(total, 0.0).astype(jnp.bfloat16)
```

```python
import functools

import jax
import jax.numpy as jnp
from jax import lax
from jax.experimental import pallas as pl
from jax.experimental.pallas import tpu as pltpu
from jax.sharding import PartitionSpec as P

BS = 128
ROWS = 8
NNZB = 44
WIDTH = 256
CHUNK = 8
LIST = 48
PHASES = ((0, 1, 2, 3, 4, 8), (5, 6, 7, 9, 10, 11))


def unpack(words):
    column = jnp.right_shift(words, 2).astype(jnp.float32).astype(jnp.bfloat16)
    value = jnp.bitwise_and(words, 3).astype(jnp.float32).astype(jnp.bfloat16)
    place = lax.broadcasted_iota(jnp.int32, (BS, BS), 0).astype(jnp.float32).astype(jnp.bfloat16)
    counts = None
    for edge in range(4):
        at = jnp.broadcast_to(column[edge : edge + 1], (BS, BS))
        much = jnp.broadcast_to(value[edge : edge + 1], (BS, BS))
        term = jnp.where(at == place, much, jnp.bfloat16(0))
        counts = term if counts is None else counts + term
    return counts


def aggregate_kernel(pieces, resumed, count_ref, list_ref, words_ref, *refs):
    parts = refs[:pieces]
    refs = refs[pieces:]
    if resumed:
        before_ref, out_ref, window, sems = refs
    else:
        out_ref, window, sems = refs
    copies = [
        pltpu.make_async_copy(part, window.at[pl.ds(i * 8 * BS, 8 * BS)], sems.at[i]) for i, part in enumerate(parts)
    ]
    for copy in copies:
        copy.start()
    for copy in copies:
        copy.wait()

    def row(r, _):
        if resumed:
            out_ref[r] = before_ref[r]
        else:
            out_ref[r] = jnp.zeros((BS, WIDTH), jnp.float32)
        count = count_ref[r]

        def chunk(c, _):
            left = []
            right = []
            for u in range(CHUNK):
                entry = c * CHUNK + u
                code = list_ref[r, entry]
                words = words_ref[r, lax.shift_right_logical(code, 7)]
                words = jnp.where(entry < count, words, 0)
                left.append(unpack(words))
                block = jnp.bitwise_and(code, 127)
                right.append(window[pl.ds(pl.multiple_of(block * BS, BS), BS), :])
            left = jnp.concatenate(left, axis=0)
            right = jnp.concatenate(right, axis=0)
            out_ref[r] += lax.dot_general(left, right, (((0,), (0,)), ((), ())), preferred_element_type=jnp.float32)
            return 0

        lax.fori_loop(0, (count + CHUNK - 1) // CHUNK, chunk, 0)
        return 0

    lax.fori_loop(0, ROWS, row, 0)


def aggregate(count, entries, words, parts, before):
    smem = pl.BlockSpec(memory_space=pltpu.SMEM)
    vmem = pl.BlockSpec(memory_space=pltpu.VMEM)
    resumed = before is not None
    return pl.pallas_call(
        functools.partial(aggregate_kernel, len(parts), resumed),
        out_shape=jax.ShapeDtypeStruct((ROWS, BS, WIDTH), jnp.float32),
        in_specs=[smem, smem, vmem] + [pl.BlockSpec(memory_space=pl.ANY)] * len(parts) + [vmem] * resumed,
        out_specs=vmem,
        scratch_shapes=[
            pltpu.VMEM((len(parts) * 8 * BS, WIDTH), jnp.bfloat16),
            pltpu.SemaphoreType.DMA((len(parts),)),
        ],
        compiler_params=pltpu.CompilerParams(vmem_limit_bytes=40 * 2**20),
        cost_estimate=pl.CostEstimate(flops=4 * 2**28 * len(parts), bytes_accessed=2**22, transcendentals=0),
        name="aggregate",
    )(count, entries, words, *parts, *([before] if resumed else []))


def finish_kernel(own_ref, sent_ref, degree_ref, features_ref, self_ref, neigh_ref, bias_ref, out_ref):
    degree = jnp.maximum(degree_ref[...], 1.0).T
    for r in range(ROWS):
        at = pl.ds(r * BS, BS)
        mean = ((own_ref[r] + sent_ref[r]) / degree[:, r : r + 1]).astype(jnp.bfloat16)
        total = jnp.dot(features_ref[at, :], self_ref[...], preferred_element_type=jnp.float32)
        total = total + jnp.dot(mean, neigh_ref[...], preferred_element_type=jnp.float32) + bias_ref[...]
        out_ref[at, :] = jnp.maximum(total, 0.0).astype(jnp.bfloat16)


def finish(own, sent, degree, features, w_self, w_neigh, bias):
    vmem = pl.BlockSpec(memory_space=pltpu.VMEM)
    return pl.pallas_call(
        finish_kernel,
        out_shape=jax.ShapeDtypeStruct((ROWS * BS, WIDTH), jnp.bfloat16),
        in_specs=[vmem] * 7,
        out_specs=vmem,
        compiler_params=pltpu.CompilerParams(vmem_limit_bytes=16 * 2**20),
        cost_estimate=pl.CostEstimate(flops=2**28, bytes_accessed=2**22, transcendentals=0),
        name="finish",
    )(own, sent, degree, features, w_self, w_neigh, bias.reshape(1, -1))


def lists(cols):
    loop, group = lax.axis_size("blk"), lax.axis_size("rep")
    mine, rep = lax.axis_index("blk"), lax.axis_index("rep")
    side = (cols // (group * ROWS) - mine + loop) % loop
    side = jnp.where(side == loop - 1, 1, jnp.where(side == 1, 2, side))
    owner = cols // ROWS % group
    away = (owner // 2 - rep // 2 + group // 2) % (group // 2)
    piece = jnp.where(owner % 2 == rep % 2, side * (group // 2) + away, -1)
    out = []
    slot = jnp.arange(NNZB, dtype=jnp.int32)
    for phase in PHASES:
        place = jnp.full(cols.shape, -1, jnp.int32)
        for i, p in enumerate(phase):
            place = jnp.where(piece == p, i, place)
        held = place >= 0
        code = slot * 128 + place * 8 + cols % ROWS
        rank = jnp.sum(held[:, None, :] & (slot[None, None, :] < slot[None, :, None]), axis=2, dtype=jnp.int32)
        spot = jnp.arange(LIST, dtype=jnp.int32)
        hit = held[:, None, :] & (rank[:, None, :] == spot[None, :, None])
        entries = jnp.sum(jnp.where(hit, code[:, None, :], 0), axis=2, dtype=jnp.int32)
        out.append((jnp.sum(held, axis=1, dtype=jnp.int32), entries))
    return out


def shards(features, block_cols, adjacency, w_self, w_neigh, bias):
    devices, loop = lax.axis_size("rep"), lax.axis_size("blk")
    sibling = [(r, r ^ 1) for r in range(devices)]
    away = [[(r, (r - 2 * d) % devices) for r in range(devices)] for d in range(4)]
    up = [(i, (i + 1) % loop) for i in range(loop)]
    down = [(j, i) for i, j in up]

    noted = jnp.pad(block_cols[:, None, None, :], ((0, 0), (0, 0), (0, 3), (0, BS - NNZB)))
    words = jnp.concatenate([adjacency, noted], axis=1)
    theirs = lax.ppermute(words, "rep", sibling)
    own = [features] + [lax.ppermute(features, "rep", away[d]) for d in (1, 3, 2)]
    own = [own[0], own[1], own[3], own[2]]
    before = [lax.ppermute(part, "blk", up) for part in own]
    after = [lax.ppermute(part, "blk", down) for part in own]
    pieces = own + before + after

    mine_lists = lists(block_cols)
    their_lists = lists(theirs[:, NNZB, 0, :NNZB])
    degree = jnp.sum(jnp.bitwise_and(adjacency, 3), axis=(1, 2)).astype(jnp.float32)

    sums = []
    for w, entries in ((theirs, their_lists), (words, mine_lists)):
        total = None
        for phase, (count, listed) in zip(PHASES, entries):
            total = aggregate(count, listed, w, [pieces[p] for p in phase], total)
        sums.append(total)
    sent = lax.ppermute(sums[0], "rep", sibling)
    return finish(sums[1], sent, degree, features, w_self, w_neigh, bias)


def solution(mesh):
    in_specs = (
        P(("blk", "rep"), None),
        P(("blk", "rep"), None),
        P(("blk", "rep"), None, None, None),
        P(),
        P(),
        P(),
    )
    out_specs = P(("blk", "rep"), None)
    return jax.shard_map(shards, mesh=mesh, in_specs=in_specs, out_specs=out_specs, check_vma=False)
```

```python
import functools

import jax
import jax.numpy as jnp
from jax import lax
from jax.experimental import pallas as pl
from jax.experimental.pallas import tpu as pltpu
from jax.sharding import PartitionSpec as P

BS = 128
ROWS = 8
NNZB = 44
WIDTH = 256
CODED = 4 * NNZB


def unpack(words):
    column = jnp.right_shift(words, 2).astype(jnp.float32).astype(jnp.bfloat16)
    value = jnp.bitwise_and(words, 3).astype(jnp.float32).astype(jnp.bfloat16)
    place = lax.broadcasted_iota(jnp.int32, (BS, BS), 0).astype(jnp.float32).astype(jnp.bfloat16)
    counts = None
    for edge in range(4):
        at = jnp.broadcast_to(column[edge : edge + 1], (BS, BS))
        much = jnp.broadcast_to(value[edge : edge + 1], (BS, BS))
        term = jnp.where(at == place, much, jnp.bfloat16(0))
        counts = term if counts is None else counts + term
    return counts


def total_of(before_ref, r, value):
    return value if before_ref is None else before_ref[r] + value


def aggregate_kernel(sources, kinds, width, together, pieces, resumed, narrow, list_ref, *refs):
    words = refs[:sources]
    parts = refs[sources : sources + pieces]
    refs = refs[sources + pieces :]
    befores = [None] * sources
    if resumed:
        befores, refs = refs[:sources], refs[sources:]
    outs, refs = refs[:sources], refs[sources:]
    totals = outs
    if narrow:
        totals, refs = [refs[0].at[i] for i in range(sources)], refs[1:]
    window, coded, sems = refs
    copies = []
    for i, ref in enumerate(parts):
        to = window.at[pl.ds(i * 8 * BS, 8 * BS)]
        copies.append(pltpu.make_async_copy(ref, to, sems.at[i]))
    for copy in copies:
        copy.start()
    for source in range(sources):
        for r in range(ROWS):
            coded[source, r] = words[source][r, :CODED, :].astype(jnp.int32)
    for copy in copies:
        copy.wait()

    for source in range(sources):
        out_ref = totals[source]
        kind = kinds[source]

        def chunk(r, c):
            count = list_ref[r, kind, BS - 1]
            left = []
            right = []
            for u in range(width):
                entry = c * width + u
                code = list_ref[r, kind, entry]
                at = pl.multiple_of(lax.shift_right_logical(code, 7) * 4, 4)
                some = jnp.where(entry < count, coded[source, r, pl.ds(at, 4), :], 0)
                left.append(unpack(some))
                block = jnp.bitwise_and(code, 127)
                right.append(window[pl.ds(pl.multiple_of(block * BS, BS), BS), :])
            left = jnp.concatenate(left, axis=0)
            right = jnp.concatenate(right, axis=0)
            return lax.dot_general(left, right, (((0,), (0,)), ((), ())), preferred_element_type=jnp.float32)

        def rows(i, _):
            for j in range(together):
                r = i * together + j
                out_ref[r] = total_of(befores[source], r, chunk(r, 0))
            for j in range(together):
                r = i * together + j

                def more(c, _):
                    out_ref[r] += chunk(r, c)
                    return 0

                lax.fori_loop(1, (list_ref[r, kind, BS - 1] + width - 1) // width, more, 0)
            return 0

        lax.fori_loop(0, ROWS // together, rows, 0)
        if narrow:
            lane = lax.broadcasted_iota(jnp.int32, (BS, BS), 1)
            scales = jnp.zeros((BS, BS), jnp.float32)
            for r in range(ROWS):
                value = out_ref[r]
                most = jnp.max(jnp.abs(value), axis=1, keepdims=True)
                power = jnp.ceil(jnp.log2(jnp.maximum(most, 2.0**-100))) - 14.0
                whole = jnp.round(value * jnp.exp2(-power))
                whole = jnp.clip(whole, -32767.0, 32767.0).astype(jnp.int32)
                outs[source][pl.ds(r * BS, BS), :] = whole.astype(jnp.int16)
                scales = jnp.where(lane == r, power, scales)
            tail = jnp.concatenate([scales.T[:16], jnp.zeros((16, BS), jnp.float32)], axis=1)
            outs[source][pl.ds(ROWS * BS, 16), :] = tail.astype(jnp.int32).astype(jnp.int16)


def aggregate(listed, words, kinds, parts, width, together, before=None, narrow=False):
    vmem = pl.BlockSpec(memory_space=pltpu.VMEM)
    whole = pl.BlockSpec(memory_space=pl.ANY)
    sources, pieces = len(words), len(parts)
    before = before or []
    shape = jax.ShapeDtypeStruct((ROWS, BS, WIDTH), jnp.float32)
    scratch = []
    if narrow:
        shape = jax.ShapeDtypeStruct((ROWS * BS + 16, WIDTH), jnp.int16)
        scratch = [pltpu.VMEM((sources, ROWS, BS, WIDTH), jnp.float32)]
    return pl.pallas_call(
        functools.partial(aggregate_kernel, sources, kinds, width, together, pieces, bool(before), narrow),
        out_shape=[shape] * sources,
        in_specs=[pl.BlockSpec(memory_space=pltpu.SMEM)] + [vmem] * sources + [whole] * pieces + [vmem] * len(before),
        out_specs=[vmem] * sources,
        scratch_shapes=scratch
        + [
            pltpu.VMEM((pieces * 8 * BS, WIDTH), jnp.bfloat16),
            pltpu.VMEM((sources, ROWS, CODED, BS), jnp.int32),
            pltpu.SemaphoreType.DMA((pieces,)),
        ],
        compiler_params=pltpu.CompilerParams(vmem_limit_bytes=40 * 2**20),
        cost_estimate=pl.CostEstimate(flops=5 * 2**30 * sources, bytes_accessed=2**23, transcendentals=0),
        name="aggregate",
    )(listed, *words, *parts, *before)


def finish_kernel(own_ref, up_ref, down_ref, degree_ref, features_ref, self_ref, neigh_ref, bias_ref, out_ref):
    degree = jnp.maximum(degree_ref[...], 1.0).T
    scales = []
    for ref in (up_ref, down_ref):
        tail = ref[pl.ds(ROWS * BS, 16), :BS].astype(jnp.int32).astype(jnp.float32)
        scales.append(jnp.exp2(tail[:ROWS]).T)
    for r in range(ROWS):
        at = pl.ds(r * BS, BS)
        total = own_ref[r]
        for ref, scale in zip((up_ref, down_ref), scales):
            total = total + ref[at, :].astype(jnp.int32).astype(jnp.float32) * scale[:, r : r + 1]
        mean = (total / degree[:, r : r + 1]).astype(jnp.bfloat16)
        total = jnp.dot(features_ref[at, :], self_ref[...], preferred_element_type=jnp.float32)
        total = total + jnp.dot(mean, neigh_ref[...], preferred_element_type=jnp.float32) + bias_ref[...]
        out_ref[at, :] = jnp.maximum(total, 0.0).astype(jnp.bfloat16)


def finish(own, up, down, degree, features, w_self, w_neigh, bias):
    vmem = pl.BlockSpec(memory_space=pltpu.VMEM)
    return pl.pallas_call(
        finish_kernel,
        out_shape=jax.ShapeDtypeStruct((ROWS * BS, WIDTH), jnp.bfloat16),
        in_specs=[vmem] * 8,
        out_specs=vmem,
        compiler_params=pltpu.CompilerParams(vmem_limit_bytes=16 * 2**20),
        cost_estimate=pl.CostEstimate(flops=2**28, bytes_accessed=2**22, transcendentals=0),
        name="finish",
    )(own, up, down, degree, features, w_self, w_neigh, bias.reshape(1, -1))


def lists(cols):
    loop, group = lax.axis_size("blk"), lax.axis_size("rep")
    mine, rep = lax.axis_index("blk"), lax.axis_index("rep")
    owner = cols // ROWS % group
    away = (owner // 2 - rep // 2 + group // 2) % (group // 2)
    other = owner % 2 != rep % 2
    side = (cols // (ROWS * group) - mine + loop) % loop
    late = away == 2
    slot = jnp.arange(NNZB, dtype=jnp.int32)
    base = slot * 128 + cols % ROWS
    order = jnp.where(late, 3, jnp.where(away == 3, 2, away))
    below, above, here = side == loop - 1, side == 1, side == 0
    kind = jnp.where(here, 4, jnp.where(above, 2, 0) + late.astype(jnp.int32))
    kind = jnp.where(below | above | here, kind, 5)
    place = jnp.where(here, order + jnp.where(other, 4, 0), order + jnp.where(other, 3, 0))
    place = jnp.where(late & ~here, jnp.where(other, 1, 0), place)
    code = base + place * 8
    ahead = slot[None, :] < slot[:, None]
    rank = jnp.sum(((kind[:, None, :] == kind[:, :, None]) & ahead).astype(jnp.int32), axis=2)
    spot = jnp.arange(5 * BS, dtype=jnp.int32)
    hit = (kind * BS + rank)[:, None, :] == spot[:, None]
    counted = (kind[:, None, :] == (spot // BS)[:, None]) & (spot % BS == BS - 1)[:, None]
    entries = jnp.sum(jnp.where(hit, code[:, None, :], 0) + counted.astype(jnp.int32), axis=2)
    return entries.reshape(ROWS, 5, BS)


def shards(features, block_cols, adjacency, w_self, w_neigh, bias):
    devices, loop = lax.axis_size("rep"), lax.axis_size("blk")
    sibling = [(r, r ^ 1) for r in range(devices)]
    away = [[(r, (r - 2 * d) % devices) for r in range(devices)] for d in range(4)]
    up = [(i, (i + 1) % loop) for i in range(loop)]
    down = [(j, i) for i, j in up]

    one = lax.ppermute(features, "rep", away[1])
    three = lax.ppermute(features, "rep", away[3])
    mine = lists(block_cols)
    words = jnp.concatenate([adjacency.reshape(ROWS, CODED, BS), jnp.pad(mine, ((0, 0), (0, 11), (0, 0)))], axis=1)
    words = words.astype(jnp.int16)
    upper = lax.ppermute(words, "blk", down)
    lower = lax.ppermute(words, "blk", up)
    listed = jnp.concatenate([upper[:, CODED : CODED + 2], lower[:, CODED + 2 : CODED + 4]], axis=1).astype(jnp.int32)
    listed = jnp.concatenate([listed, mine[:, 4:5]], axis=1)
    half = features.shape[0] // 2
    ahead = lax.ppermute(one[:half], "rep", away[1])
    behind = lax.ppermute(three[half:], "rep", away[3])
    early = [features, one, three]
    early = early + [lax.ppermute(part, "rep", sibling) for part in early]
    sums = aggregate(listed, [upper, lower], (0, 2), early, 12, 2)
    ahead, behind, *sums = lax.optimization_barrier((ahead, behind, *sums))
    two = jnp.concatenate([ahead, behind], axis=0)
    late = [two, lax.ppermute(two, "rep", sibling)]
    for_upper, for_lower = aggregate(listed, [upper, lower], (1, 3), late, 8, 4, sums, True)
    from_below = lax.ppermute(for_upper, "blk", up)
    from_above = lax.ppermute(for_lower, "blk", down)
    pieces = early[:3] + late[:1] + early[3:] + late[1:]
    coded, _ = lax.optimization_barrier((adjacency, for_upper))
    degree = jnp.sum(jnp.bitwise_and(coded, 3), axis=(1, 2)).astype(jnp.float32)
    (mine,) = aggregate(listed, [words], (4,), pieces, 16, 2)
    return finish(mine, from_below, from_above, degree, features, w_self, w_neigh, bias)


def solution(mesh):
    in_specs = (
        P(("blk", "rep"), None),
        P(("blk", "rep"), None),
        P(("blk", "rep"), None, None, None),
        P(),
        P(),
        P(),
    )
    out_specs = P(("blk", "rep"), None)
    return jax.shard_map(shards, mesh=mesh, in_specs=in_specs, out_specs=out_specs, check_vma=False)
```

```python
import functools

import jax
import jax.numpy as jnp
from jax import lax
from jax.experimental import pallas as pl
from jax.experimental.pallas import tpu as pltpu
from jax.sharding import PartitionSpec as P

BS = 128
ROWS = 8
NNZB = 44
WIDTH = 256
CODED = 4 * NNZB


def unpack(words):
    column = jnp.right_shift(words, 2).astype(jnp.float32).astype(jnp.bfloat16)
    value = jnp.bitwise_and(words, 3).astype(jnp.float32).astype(jnp.bfloat16)
    place = lax.broadcasted_iota(jnp.int32, (BS, BS), 0).astype(jnp.float32).astype(jnp.bfloat16)
    counts = None
    for edge in range(4):
        at = jnp.broadcast_to(column[edge : edge + 1], (BS, BS))
        much = jnp.broadcast_to(value[edge : edge + 1], (BS, BS))
        term = jnp.where(at == place, much, jnp.bfloat16(0))
        counts = term if counts is None else counts + term
    return counts


def total_of(before_ref, r, value):
    return value if before_ref is None else before_ref[r] + value


def aggregate_kernel(sources, kinds, width, together, pieces, resumed, narrow, *refs):
    words = refs[:sources]
    parts = refs[sources : sources + pieces]
    refs = refs[sources + pieces :]
    befores = [None] * sources
    if resumed:
        befores, refs = refs[:sources], refs[sources:]
    outs, refs = refs[:sources], refs[sources:]
    totals = outs
    if narrow:
        totals, refs = [refs[0].at[i] for i in range(sources)], refs[1:]
    window, coded, noted, lists_ref, sems = refs
    copies = []
    at = 0
    for i, ref in enumerate(parts):
        copies.append(pltpu.make_async_copy(ref, window.at[pl.ds(at, ref.shape[0])], sems.at[i]))
        at += ref.shape[0]
    for copy in copies:
        copy.start()
    for source in range(sources):
        for r in range(ROWS):
            noted[source, r] = words[source][r, CODED:, :].astype(jnp.int32)
    scalars = pltpu.make_async_copy(noted.at[:, :, pl.ds(0, 8)], lists_ref, sems.at[pieces])
    scalars.start()
    for source in range(sources):
        for r in range(ROWS):
            coded[source, r] = words[source][r, :CODED, :].astype(jnp.int32)
    scalars.wait()
    for copy in copies:
        copy.wait()

    for source in range(sources):
        out_ref = totals[source]
        kind = kinds[source]

        def chunk(r, c):
            count = lists_ref[source, r, kind, BS - 1]
            left = []
            right = []
            for u in range(width):
                entry = c * width + u
                code = lists_ref[source, r, kind, entry]
                at = pl.multiple_of(lax.shift_right_logical(code, 7) * 4, 4)
                some = jnp.where(entry < count, coded[source, r, pl.ds(at, 4), :], 0)
                left.append(unpack(some))
                block = jnp.bitwise_and(code, 127)
                right.append(window[pl.ds(pl.multiple_of(block * BS, BS), BS), :])
            left = jnp.concatenate(left, axis=0)
            right = jnp.concatenate(right, axis=0)
            return lax.dot_general(left, right, (((0,), (0,)), ((), ())), preferred_element_type=jnp.float32)

        def rows(i, _):
            for j in range(together):
                r = i * together + j
                out_ref[r] = total_of(befores[source], r, chunk(r, 0))
            for j in range(together):
                r = i * together + j

                def more(c, _):
                    out_ref[r] += chunk(r, c)
                    return 0

                lax.fori_loop(1, (lists_ref[source, r, kind, BS - 1] + width - 1) // width, more, 0)
            return 0

        lax.fori_loop(0, ROWS // together, rows, 0)
        if narrow:
            lane = lax.broadcasted_iota(jnp.int32, (BS, BS), 1)
            scales = jnp.zeros((BS, BS), jnp.float32)
            for r in range(ROWS):
                value = out_ref[r]
                most = jnp.max(jnp.abs(value), axis=1, keepdims=True)
                power = jnp.ceil(jnp.log2(jnp.maximum(most, 2.0**-100))) - 14.0
                whole = jnp.round(value * jnp.exp2(-power))
                whole = jnp.clip(whole, -32767.0, 32767.0).astype(jnp.int32)
                outs[source][pl.ds(r * BS, BS), :] = whole.astype(jnp.int16)
                scales = jnp.where(lane == r, power, scales)
            tail = jnp.concatenate([scales.T[:16], jnp.zeros((16, BS), jnp.float32)], axis=1)
            outs[source][pl.ds(ROWS * BS, 16), :] = tail.astype(jnp.int32).astype(jnp.int16)


def aggregate(words, kinds, parts, width, together, before=None, narrow=False):
    vmem = pl.BlockSpec(memory_space=pltpu.VMEM)
    whole = pl.BlockSpec(memory_space=pl.ANY)
    sources, pieces = len(words), len(parts)
    before = before or []
    shape = jax.ShapeDtypeStruct((ROWS, BS, WIDTH), jnp.float32)
    scratch = []
    if narrow:
        shape = jax.ShapeDtypeStruct((ROWS * BS + 16, WIDTH), jnp.int16)
        scratch = [pltpu.VMEM((sources, ROWS, BS, WIDTH), jnp.float32)]
    return pl.pallas_call(
        functools.partial(aggregate_kernel, sources, kinds, width, together, pieces, bool(before), narrow),
        out_shape=[shape] * sources,
        in_specs=[vmem] * sources + [whole] * pieces + [vmem] * len(before),
        out_specs=[vmem] * sources,
        scratch_shapes=scratch
        + [
            pltpu.VMEM((sum(part.shape[0] for part in parts), WIDTH), jnp.bfloat16),
            pltpu.VMEM((sources, ROWS, CODED, BS), jnp.int32),
            pltpu.VMEM((sources, ROWS, 16, BS), jnp.int32),
            pltpu.SMEM((sources, ROWS, 8, BS), jnp.int32),
            pltpu.SemaphoreType.DMA((pieces + 1,)),
        ],
        compiler_params=pltpu.CompilerParams(vmem_limit_bytes=40 * 2**20),
        cost_estimate=pl.CostEstimate(flops=0, bytes_accessed=0, transcendentals=0),
        name="aggregate",
    )(*words, *parts, *before)


def finish_kernel(own_ref, up_ref, down_ref, degree_ref, features_ref, self_ref, neigh_ref, bias_ref, out_ref):
    degree = jnp.maximum(degree_ref[...], 1.0).T
    scales = []
    for ref in (up_ref, down_ref):
        tail = ref[pl.ds(ROWS * BS, 16), :BS].astype(jnp.int32).astype(jnp.float32)
        scales.append(jnp.exp2(tail[:ROWS]).T)
    for r in range(ROWS):
        at = pl.ds(r * BS, BS)
        total = own_ref[r]
        for ref, scale in zip((up_ref, down_ref), scales):
            total = total + ref[at, :].astype(jnp.int32).astype(jnp.float32) * scale[:, r : r + 1]
        mean = (total / degree[:, r : r + 1]).astype(jnp.bfloat16)
        total = jnp.dot(features_ref[at, :], self_ref[...], preferred_element_type=jnp.float32)
        total = total + jnp.dot(mean, neigh_ref[...], preferred_element_type=jnp.float32) + bias_ref[...]
        out_ref[at, :] = jnp.maximum(total, 0.0).astype(jnp.bfloat16)


def finish(own, up, down, degree, features, w_self, w_neigh, bias):
    vmem = pl.BlockSpec(memory_space=pltpu.VMEM)
    return pl.pallas_call(
        finish_kernel,
        out_shape=jax.ShapeDtypeStruct((ROWS * BS, WIDTH), jnp.bfloat16),
        in_specs=[vmem] * 8,
        out_specs=vmem,
        compiler_params=pltpu.CompilerParams(vmem_limit_bytes=16 * 2**20),
        cost_estimate=pl.CostEstimate(flops=2**28, bytes_accessed=2**22, transcendentals=0),
        name="finish",
    )(own, up, down, degree, features, w_self, w_neigh, bias.reshape(1, -1))


def lists(cols):
    loop, group = lax.axis_size("blk"), lax.axis_size("rep")
    mine, rep = lax.axis_index("blk"), lax.axis_index("rep")
    owner = cols // ROWS % group
    away = (owner // 2 - rep // 2 + group // 2) % (group // 2)
    other = owner % 2 != rep % 2
    side = (cols // (ROWS * group) - mine + loop) % loop
    slot = jnp.arange(NNZB, dtype=jnp.int32)
    base = slot * 128 + cols % ROWS
    late = (away == 2) | (other & (away != 0))
    place = jnp.where(away == 0, 0, jnp.where(away == 1, 2, 3)) + jnp.where(other, 1, 0)
    place = jnp.where(late, jnp.where(away == 2, 4, jnp.where(away == 1, 5, 6)) + jnp.where(other, 1, 0), place)
    below, above, here = side == loop - 1, side == 1, side == 0
    kind = jnp.where(here, 4, jnp.where(above, 2, 0) + late.astype(jnp.int32))
    kind = jnp.where(below | above | here, kind, 5)
    place = jnp.where(late & ~here, place - 4, place)
    code = base + place * 8
    ahead = slot[None, :] < slot[:, None]
    rank = jnp.sum(((kind[:, None, :] == kind[:, :, None]) & ahead).astype(jnp.int32), axis=2)
    spot = jnp.arange(5 * BS, dtype=jnp.int32)
    hit = (kind * BS + rank)[:, None, :] == spot[:, None]
    counted = (kind[:, None, :] == (spot // BS)[:, None]) & (spot % BS == BS - 1)[:, None]
    entries = jnp.sum(jnp.where(hit, code[:, None, :], 0) + counted.astype(jnp.int32), axis=2)
    return entries.reshape(ROWS, 5, BS)


def shards(features, block_cols, adjacency, w_self, w_neigh, bias):
    devices, loop = lax.axis_size("rep"), lax.axis_size("blk")
    sibling = [(r, r ^ 1) for r in range(devices)]
    away = [[(r, (r - 2 * d) % devices) for r in range(devices)] for d in range(4)]
    up = [(i, (i + 1) % loop) for i in range(loop)]
    down = [(j, i) for i, j in up]

    one = lax.ppermute(features, "rep", away[1])
    three = lax.ppermute(features, "rep", away[3])
    mine = lists(block_cols)
    words = jnp.concatenate([adjacency.reshape(ROWS, CODED, BS), jnp.pad(mine, ((0, 0), (0, 11), (0, 0)))], axis=1)
    words = words.astype(jnp.int16)
    upper = lax.ppermute(words, "blk", down)
    lower = lax.ppermute(words, "blk", up)
    half = features.shape[0] // 2
    ahead = lax.ppermute(one[:half], "rep", away[1])
    behind = lax.ppermute(three[half:], "rep", away[3])
    both = jnp.concatenate([one, three], axis=0)
    sib_own = lax.ppermute(features, "rep", sibling)
    early = [features, sib_own, both]
    sums = aggregate([upper, lower], (0, 2), early, 10, 2)
    ahead, behind, *sums = lax.optimization_barrier((ahead, behind, *sums))
    two = jnp.concatenate([ahead, behind], axis=0)
    late = [two, lax.ppermute(two, "rep", sibling), lax.ppermute(both, "rep", sibling)]
    for_upper, for_lower = aggregate([upper, lower], (1, 3), late, 10, 2, sums, True)
    from_below = lax.ppermute(for_upper, "blk", up)
    from_above = lax.ppermute(for_lower, "blk", down)
    pieces = early + late
    coded, _ = lax.optimization_barrier((adjacency, for_upper))
    degree = jnp.sum(jnp.bitwise_and(coded, 3), axis=(1, 2)).astype(jnp.float32)
    (mine,) = aggregate([words], (4,), pieces, 16, 2)
    return finish(mine, from_below, from_above, degree, features, w_self, w_neigh, bias)


def solution(mesh):
    in_specs = (
        P(("blk", "rep"), None),
        P(("blk", "rep"), None),
        P(("blk", "rep"), None, None, None),
        P(),
        P(),
        P(),
    )
    out_specs = P(("blk", "rep"), None)
    return jax.shard_map(shards, mesh=mesh, in_specs=in_specs, out_specs=out_specs, check_vma=False)
```

```python
import functools

import jax
import jax.numpy as jnp
from jax import lax
from jax.experimental import pallas as pl
from jax.experimental.pallas import tpu as pltpu
from jax.sharding import PartitionSpec as P

BS = 128
ROWS = 8
NNZB = 44
WIDTH = 256
CODED = 4 * NNZB


def unpack(words):
    column = jnp.right_shift(words, 2).astype(jnp.float32).astype(jnp.bfloat16)
    value = jnp.bitwise_and(words, 3).astype(jnp.float32).astype(jnp.bfloat16)
    place = lax.broadcasted_iota(jnp.int32, (BS, BS), 0).astype(jnp.float32).astype(jnp.bfloat16)
    counts = None
    for edge in range(4):
        at = jnp.broadcast_to(column[edge : edge + 1], (BS, BS))
        much = jnp.broadcast_to(value[edge : edge + 1], (BS, BS))
        term = jnp.where(at == place, much, jnp.bfloat16(0))
        counts = term if counts is None else counts + term
    return counts


def total_of(before_ref, r, value):
    return value if before_ref is None else before_ref[r] + value


def aggregate_kernel(sources, kinds, width, together, pieces, resumed, narrow, *refs):
    words = refs[:sources]
    parts = refs[sources : sources + pieces]
    refs = refs[sources + pieces :]
    befores = [None] * sources
    if resumed:
        befores, refs = refs[:sources], refs[sources:]
    outs, refs = refs[:sources], refs[sources:]
    totals = outs
    if narrow:
        totals, refs = [refs[0].at[i] for i in range(sources)], refs[1:]
    window, coded, noted, lists_ref, sems = refs
    copies = []
    at = 0
    for i, ref in enumerate(parts):
        copies.append(pltpu.make_async_copy(ref, window.at[pl.ds(at, ref.shape[0])], sems.at[i]))
        at += ref.shape[0]
    for copy in copies:
        copy.start()
    for source in range(sources):
        for r in range(ROWS):
            noted[source, r] = words[source][r, CODED:, :].astype(jnp.int32)
    scalars = [
        pltpu.make_async_copy(noted.at[source, :, kinds[source]], lists_ref.at[source], sems.at[pieces + source])
        for source in range(sources)
    ]
    for copy in scalars:
        copy.start()
    for source in range(sources):
        for r in range(ROWS):
            coded[source, r] = words[source][r, :CODED, :].astype(jnp.int32)
    for copy in scalars + copies:
        copy.wait()

    for source in range(sources):
        out_ref = totals[source]

        def chunk(r, c):
            count = lists_ref[source, r, BS - 1]
            left = []
            right = []
            for u in range(width):
                entry = c * width + u
                code = lists_ref[source, r, entry]
                at = pl.multiple_of(lax.shift_right_logical(code, 7) * 4, 4)
                some = jnp.where(entry < count, coded[source, r, pl.ds(at, 4), :], 0)
                left.append(unpack(some))
                block = jnp.bitwise_and(code, 127)
                right.append(window[pl.ds(pl.multiple_of(block * BS, BS), BS), :])
            left = jnp.concatenate(left, axis=0)
            right = jnp.concatenate(right, axis=0)
            return lax.dot_general(left, right, (((0,), (0,)), ((), ())), preferred_element_type=jnp.float32)

        def rows(i, _):
            for j in range(together):
                r = i * together + j
                out_ref[r] = total_of(befores[source], r, chunk(r, 0))
            for j in range(together):
                r = i * together + j

                def more(c, _):
                    out_ref[r] += chunk(r, c)
                    return 0

                lax.fori_loop(1, (lists_ref[source, r, BS - 1] + width - 1) // width, more, 0)
            return 0

        lax.fori_loop(0, ROWS // together, rows, 0)
        if narrow:
            lane = lax.broadcasted_iota(jnp.int32, (BS, BS), 1)
            scales = jnp.zeros((BS, BS), jnp.float32)
            for r in range(ROWS):
                value = out_ref[r]
                most = jnp.max(jnp.abs(value), axis=1, keepdims=True)
                power = jnp.ceil(jnp.log2(jnp.maximum(most, 2.0**-100))) - 14.0
                whole = jnp.round(value * jnp.exp2(-power))
                whole = jnp.clip(whole, -32767.0, 32767.0).astype(jnp.int32)
                outs[source][pl.ds(r * BS, BS), :] = whole.astype(jnp.int16)
                scales = jnp.where(lane == r, power, scales)
            tail = jnp.concatenate([scales.T[:16], jnp.zeros((16, BS), jnp.float32)], axis=1)
            outs[source][pl.ds(ROWS * BS, 16), :] = tail.astype(jnp.int32).astype(jnp.int16)


def aggregate(words, kinds, parts, width, together, before=None, narrow=False):
    vmem = pl.BlockSpec(memory_space=pltpu.VMEM)
    whole = pl.BlockSpec(memory_space=pl.ANY)
    sources, pieces = len(words), len(parts)
    before = before or []
    shape = jax.ShapeDtypeStruct((ROWS, BS, WIDTH), jnp.float32)
    scratch = []
    if narrow:
        shape = jax.ShapeDtypeStruct((ROWS * BS + 16, WIDTH), jnp.int16)
        scratch = [pltpu.VMEM((sources, ROWS, BS, WIDTH), jnp.float32)]
    return pl.pallas_call(
        functools.partial(aggregate_kernel, sources, kinds, width, together, pieces, bool(before), narrow),
        out_shape=[shape] * sources,
        in_specs=[vmem] * sources + [whole] * pieces + [vmem] * len(before),
        out_specs=[vmem] * sources,
        scratch_shapes=scratch
        + [
            pltpu.VMEM((sum(part.shape[0] for part in parts), WIDTH), jnp.bfloat16),
            pltpu.VMEM((sources, ROWS, CODED, BS), jnp.int32),
            pltpu.VMEM((sources, ROWS, 16, BS), jnp.int32),
            pltpu.SMEM((sources, ROWS, BS), jnp.int32),
            pltpu.SemaphoreType.DMA((pieces + sources,)),
        ],
        compiler_params=pltpu.CompilerParams(vmem_limit_bytes=40 * 2**20),
        cost_estimate=pl.CostEstimate(flops=0, bytes_accessed=0, transcendentals=0),
        name="aggregate",
    )(*words, *parts, *before)


def finish_kernel(own_ref, up_ref, down_ref, degree_ref, features_ref, self_ref, neigh_ref, bias_ref, out_ref):
    degree = jnp.maximum(degree_ref[...], 1.0).T
    scales = []
    for ref in (up_ref, down_ref):
        tail = ref[pl.ds(ROWS * BS, 16), :BS].astype(jnp.int32).astype(jnp.float32)
        scales.append(jnp.exp2(tail[:ROWS]).T)
    for r in range(ROWS):
        at = pl.ds(r * BS, BS)
        total = own_ref[r]
        for ref, scale in zip((up_ref, down_ref), scales):
            total = total + ref[at, :].astype(jnp.int32).astype(jnp.float32) * scale[:, r : r + 1]
        mean = (total / degree[:, r : r + 1]).astype(jnp.bfloat16)
        total = jnp.dot(features_ref[at, :], self_ref[...], preferred_element_type=jnp.float32)
        total = total + jnp.dot(mean, neigh_ref[...], preferred_element_type=jnp.float32) + bias_ref[...]
        out_ref[at, :] = jnp.maximum(total, 0.0).astype(jnp.bfloat16)


def finish(own, up, down, degree, features, w_self, w_neigh, bias):
    vmem = pl.BlockSpec(memory_space=pltpu.VMEM)
    return pl.pallas_call(
        finish_kernel,
        out_shape=jax.ShapeDtypeStruct((ROWS * BS, WIDTH), jnp.bfloat16),
        in_specs=[vmem] * 8,
        out_specs=vmem,
        compiler_params=pltpu.CompilerParams(vmem_limit_bytes=16 * 2**20),
        cost_estimate=pl.CostEstimate(flops=2**28, bytes_accessed=2**22, transcendentals=0),
        name="finish",
    )(own, up, down, degree, features, w_self, w_neigh, bias.reshape(1, -1))


def lists(cols):
    loop, group = lax.axis_size("blk"), lax.axis_size("rep")
    mine, rep = lax.axis_index("blk"), lax.axis_index("rep")
    owner = cols // ROWS % group
    away = (owner // 2 - rep // 2 + group // 2) % (group // 2)
    other = owner % 2 != rep % 2
    side = (cols // (ROWS * group) - mine + loop) % loop
    slot = jnp.arange(NNZB, dtype=jnp.int32)
    base = slot * 128 + cols % ROWS
    late = (away == 2) | (other & (away != 0))
    place = jnp.where(away == 0, 0, jnp.where(away == 1, 2, 3)) + jnp.where(other, 1, 0)
    place = jnp.where(late, jnp.where(away == 2, 4, jnp.where(away == 1, 5, 6)) + jnp.where(other, 1, 0), place)
    below, above, here = side == loop - 1, side == 1, side == 0
    kind = jnp.where(here, 4, jnp.where(above, 2, 0) + late.astype(jnp.int32))
    kind = jnp.where(below | above | here, kind, 5)
    place = jnp.where(late & ~here, place - 4, place)
    code = base + place * 8
    ahead = slot[None, :] < slot[:, None]
    rank = jnp.sum(((kind[:, None, :] == kind[:, :, None]) & ahead).astype(jnp.int32), axis=2)
    spot = jnp.arange(5 * BS, dtype=jnp.int32)
    hit = (kind * BS + rank)[:, None, :] == spot[:, None]
    counted = (kind[:, None, :] == (spot // BS)[:, None]) & (spot % BS == BS - 1)[:, None]
    entries = jnp.sum(jnp.where(hit, code[:, None, :], 0) + counted.astype(jnp.int32), axis=2)
    return entries.reshape(ROWS, 5, BS)


def shards(features, block_cols, adjacency, w_self, w_neigh, bias):
    devices, loop = lax.axis_size("rep"), lax.axis_size("blk")
    sibling = [(r, r ^ 1) for r in range(devices)]
    away = [[(r, (r - 2 * d) % devices) for r in range(devices)] for d in range(4)]
    up = [(i, (i + 1) % loop) for i in range(loop)]
    down = [(j, i) for i, j in up]

    one = lax.ppermute(features, "rep", away[1])
    three = lax.ppermute(features, "rep", away[3])
    mine = lists(block_cols)
    words = jnp.concatenate([adjacency.reshape(ROWS, CODED, BS), jnp.pad(mine, ((0, 0), (0, 11), (0, 0)))], axis=1)
    words = words.astype(jnp.int16)
    upper = lax.ppermute(words, "blk", down)
    lower = lax.ppermute(words, "blk", up)
    half = features.shape[0] // 2
    ahead = lax.ppermute(one[:half], "rep", away[1])
    behind = lax.ppermute(three[half:], "rep", away[3])
    both = jnp.concatenate([one, three], axis=0)
    sib_own = lax.ppermute(features, "rep", sibling)
    early = [features, sib_own, both]
    sums = aggregate([upper, lower], (0, 2), early, 8, 8)
    ahead, behind, *sums = lax.optimization_barrier((ahead, behind, *sums))
    two = jnp.concatenate([ahead, behind], axis=0)
    late = [two, lax.ppermute(two, "rep", sibling), lax.ppermute(both, "rep", sibling)]
    for_upper, for_lower = aggregate([upper, lower], (1, 3), late, 10, 4, sums, True)
    from_below = lax.ppermute(for_upper, "blk", up)
    from_above = lax.ppermute(for_lower, "blk", down)
    pieces = early + late
    coded, _ = lax.optimization_barrier((adjacency, for_upper))
    degree = jnp.sum(jnp.bitwise_and(coded, 3), axis=(1, 2)).astype(jnp.float32)
    (mine,) = aggregate([words], (4,), pieces, 16, 8)
    return finish(mine, from_below, from_above, degree, features, w_self, w_neigh, bias)


def solution(mesh):
    in_specs = (
        P(("blk", "rep"), None),
        P(("blk", "rep"), None),
        P(("blk", "rep"), None, None, None),
        P(),
        P(),
        P(),
    )
    out_specs = P(("blk", "rep"), None)
    return jax.shard_map(shards, mesh=mesh, in_specs=in_specs, out_specs=out_specs, check_vma=False)
```

```python
import functools

import jax
import jax.numpy as jnp
from jax import lax
from jax.experimental import pallas as pl
from jax.experimental.pallas import tpu as pltpu
from jax.sharding import PartitionSpec as P

BS = 128
ROWS = 8
NNZB = 44
WIDTH = 256
CODED = 4 * NNZB


def unpack(words):
    column = jnp.right_shift(words, 2).astype(jnp.float32).astype(jnp.bfloat16)
    value = jnp.bitwise_and(words, 3).astype(jnp.float32).astype(jnp.bfloat16)
    place = lax.broadcasted_iota(jnp.int32, (BS, BS), 0).astype(jnp.float32).astype(jnp.bfloat16)
    counts = None
    for edge in range(4):
        at = jnp.broadcast_to(column[edge : edge + 1], (BS, BS))
        much = jnp.broadcast_to(value[edge : edge + 1], (BS, BS))
        term = jnp.where(at == place, much, jnp.bfloat16(0))
        counts = term if counts is None else counts + term
    return counts


def total_of(before_ref, r, value):
    return value if before_ref is None else before_ref[r] + value


def aggregate_kernel(sources, kinds, width, together, pieces, resumed, narrow, *refs):
    words = refs[:sources]
    parts = refs[sources : sources + pieces]
    refs = refs[sources + pieces :]
    befores = [None] * sources
    if resumed:
        befores, refs = refs[:sources], refs[sources:]
    outs, refs = refs[:sources], refs[sources:]
    totals = outs
    if narrow:
        totals, refs = [refs[0].at[i] for i in range(sources)], refs[1:]
    window, coded, noted, lists_ref, sems = refs
    copies = []
    at = 0
    for i, ref in enumerate(parts):
        copies.append(pltpu.make_async_copy(ref, window.at[pl.ds(at, ref.shape[0])], sems.at[i]))
        at += ref.shape[0]
    for copy in copies:
        copy.start()
    for source in range(sources):
        for r in range(ROWS):
            noted[source, r] = words[source][r, CODED:, :].astype(jnp.int32)
    scalars = [
        pltpu.make_async_copy(noted.at[source, :, kinds[source]], lists_ref.at[source], sems.at[pieces + source])
        for source in range(sources)
    ]
    for copy in scalars:
        copy.start()
    for source in range(sources):
        for r in range(ROWS):
            coded[source, r] = words[source][r, :CODED, :].astype(jnp.int32)
    for copy in scalars + copies:
        copy.wait()

    for source in range(sources):
        out_ref = totals[source]

        def chunk(r, c):
            count = lists_ref[source, r, BS - 1]
            left = []
            right = []
            for u in range(width):
                entry = c * width + u
                code = lists_ref[source, r, entry]
                at = pl.multiple_of(lax.shift_right_logical(code, 7) * 4, 4)
                some = jnp.where(entry < count, coded[source, r, pl.ds(at, 4), :], 0)
                left.append(unpack(some))
                block = jnp.bitwise_and(code, 127)
                right.append(window[pl.ds(pl.multiple_of(block * BS, BS), BS), :])
            left = jnp.concatenate(left, axis=0)
            right = jnp.concatenate(right, axis=0)
            return lax.dot_general(left, right, (((0,), (0,)), ((), ())), preferred_element_type=jnp.float32)

        def rows(i, _):
            for j in range(together):
                r = i * together + j
                out_ref[r] = total_of(befores[source], r, chunk(r, 0))
            for j in range(together):
                r = i * together + j

                def more(c, _):
                    out_ref[r] += chunk(r, c)
                    return 0

                lax.fori_loop(1, (lists_ref[source, r, BS - 1] + width - 1) // width, more, 0)
            return 0

        lax.fori_loop(0, ROWS // together, rows, 0)
        if narrow:
            lane = lax.broadcasted_iota(jnp.int32, (BS, BS), 1)
            scales = jnp.zeros((BS, BS), jnp.float32)
            for r in range(ROWS):
                value = out_ref[r]
                most = jnp.max(jnp.abs(value), axis=1, keepdims=True)
                power = jnp.ceil(jnp.log2(jnp.maximum(most, 2.0**-100))) - 14.0
                whole = jnp.round(value * jnp.exp2(-power))
                whole = jnp.clip(whole, -32767.0, 32767.0).astype(jnp.int32)
                outs[source][pl.ds(r * BS, BS), :] = whole.astype(jnp.int16)
                scales = jnp.where(lane == r, power, scales)
            tail = jnp.concatenate([scales.T[:16], jnp.zeros((16, BS), jnp.float32)], axis=1)
            outs[source][pl.ds(ROWS * BS, 16), :] = tail.astype(jnp.int32).astype(jnp.int16)


def aggregate(words, kinds, parts, width, together, before=None, narrow=False):
    vmem = pl.BlockSpec(memory_space=pltpu.VMEM)
    whole = pl.BlockSpec(memory_space=pl.ANY)
    sources, pieces = len(words), len(parts)
    before = before or []
    shape = jax.ShapeDtypeStruct((ROWS, BS, WIDTH), jnp.float32)
    scratch = []
    if narrow:
        shape = jax.ShapeDtypeStruct((ROWS * BS + 16, WIDTH), jnp.int16)
        scratch = [pltpu.VMEM((sources, ROWS, BS, WIDTH), jnp.float32)]
    return pl.pallas_call(
        functools.partial(aggregate_kernel, sources, kinds, width, together, pieces, bool(before), narrow),
        out_shape=[shape] * sources,
        in_specs=[vmem] * sources + [whole] * pieces + [vmem] * len(before),
        out_specs=[vmem] * sources,
        scratch_shapes=scratch
        + [
            pltpu.VMEM((sum(part.shape[0] for part in parts), WIDTH), jnp.bfloat16),
            pltpu.VMEM((sources, ROWS, CODED, BS), jnp.int32),
            pltpu.VMEM((sources, ROWS, 16, BS), jnp.int32),
            pltpu.SMEM((sources, ROWS, BS), jnp.int32),
            pltpu.SemaphoreType.DMA((pieces + sources,)),
        ],
        compiler_params=pltpu.CompilerParams(vmem_limit_bytes=40 * 2**20),
        cost_estimate=pl.CostEstimate(flops=0, bytes_accessed=0, transcendentals=0),
        name="aggregate",
    )(*words, *parts, *before)


def finish_kernel(own_ref, up_ref, down_ref, degree_ref, features_ref, self_ref, neigh_ref, bias_ref, out_ref):
    degree = jnp.maximum(degree_ref[...], 1.0).T
    scales = []
    for ref in (up_ref, down_ref):
        tail = ref[pl.ds(ROWS * BS, 16), :BS].astype(jnp.int32).astype(jnp.float32)
        scales.append(jnp.exp2(tail[:ROWS]).T)
    for r in range(ROWS):
        at = pl.ds(r * BS, BS)
        total = own_ref[r]
        for ref, scale in zip((up_ref, down_ref), scales):
            total = total + ref[at, :].astype(jnp.int32).astype(jnp.float32) * scale[:, r : r + 1]
        mean = (total / degree[:, r : r + 1]).astype(jnp.bfloat16)
        total = jnp.dot(features_ref[at, :], self_ref[...], preferred_element_type=jnp.float32)
        total = total + jnp.dot(mean, neigh_ref[...], preferred_element_type=jnp.float32) + bias_ref[...]
        out_ref[at, :] = jnp.maximum(total, 0.0).astype(jnp.bfloat16)


def finish(own, up, down, degree, features, w_self, w_neigh, bias):
    vmem = pl.BlockSpec(memory_space=pltpu.VMEM)
    return pl.pallas_call(
        finish_kernel,
        out_shape=jax.ShapeDtypeStruct((ROWS * BS, WIDTH), jnp.bfloat16),
        in_specs=[vmem] * 8,
        out_specs=vmem,
        compiler_params=pltpu.CompilerParams(vmem_limit_bytes=16 * 2**20),
        cost_estimate=pl.CostEstimate(flops=2**28, bytes_accessed=2**22, transcendentals=0),
        name="finish",
    )(own, up, down, degree, features, w_self, w_neigh, bias.reshape(1, -1))


def lists(cols):
    loop, group = lax.axis_size("blk"), lax.axis_size("rep")
    mine, rep = lax.axis_index("blk"), lax.axis_index("rep")
    owner = cols // ROWS % group
    away = (owner // 2 - rep // 2 + group // 2) % (group // 2)
    other = owner % 2 != rep % 2
    side = (cols // (ROWS * group) - mine + loop) % loop
    slot = jnp.arange(NNZB, dtype=jnp.int32)
    base = slot * 128 + cols % ROWS
    late = (away == 2) | (other & (away != 0))
    place = jnp.where(away == 0, 0, jnp.where(away == 1, 2, 3)) + jnp.where(other, 1, 0)
    place = jnp.where(late, 4 + jnp.where(other, jnp.where(away == 2, 3, jnp.where(away == 1, 1, 2)), 0), place)
    below, above, here = side == loop - 1, side == 1, side == 0
    kind = jnp.where(here, 4, jnp.where(above, 2, 0) + late.astype(jnp.int32))
    kind = jnp.where(below | above | here, kind, 5)
    place = jnp.where(late & ~here, place - 4, place)
    code = base + place * 8
    ahead = slot[None, :] < slot[:, None]
    rank = jnp.sum(((kind[:, None, :] == kind[:, :, None]) & ahead).astype(jnp.int32), axis=2)
    spot = jnp.arange(5 * BS, dtype=jnp.int32)
    hit = (kind * BS + rank)[:, None, :] == spot[:, None]
    counted = (kind[:, None, :] == (spot // BS)[:, None]) & (spot % BS == BS - 1)[:, None]
    entries = jnp.sum(jnp.where(hit, code[:, None, :], 0) + counted.astype(jnp.int32), axis=2)
    return entries.reshape(ROWS, 5, BS)


def shards(features, block_cols, adjacency, w_self, w_neigh, bias):
    devices, loop = lax.axis_size("rep"), lax.axis_size("blk")
    sibling = [(r, r ^ 1) for r in range(devices)]
    away = [[(r, (r - 2 * d) % devices) for r in range(devices)] for d in range(4)]
    up = [(i, (i + 1) % loop) for i in range(loop)]
    down = [(j, i) for i, j in up]

    one = lax.ppermute(features, "rep", away[1])
    three = lax.ppermute(features, "rep", away[3])
    mine = lists(block_cols)
    words = jnp.concatenate([adjacency.reshape(ROWS, CODED, BS), jnp.pad(mine, ((0, 0), (0, 11), (0, 0)))], axis=1)
    words = words.astype(jnp.int16)
    upper = lax.ppermute(words, "blk", down)
    lower = lax.ppermute(words, "blk", up)
    half = features.shape[0] // 2
    ahead = lax.ppermute(one[:half], "rep", away[1])
    behind = lax.ppermute(three[half:], "rep", away[3])
    both = jnp.concatenate([one, three], axis=0)
    spare, words = lax.optimization_barrier((features, words))
    sib_own = lax.ppermute(spare, "rep", sibling)
    early = [features, sib_own, both]
    sums = aggregate([upper, lower], (0, 2), early, 8, 8)
    ahead, behind, *sums = lax.optimization_barrier((ahead, behind, *sums))
    two = jnp.concatenate([ahead, behind], axis=0)
    late = [two, lax.ppermute(jnp.concatenate([both, two], axis=0), "rep", sibling)]
    for_upper, for_lower = aggregate([upper, lower], (1, 3), late, 10, 4, sums, True)
    from_below = lax.ppermute(for_upper, "blk", up)
    from_above = lax.ppermute(for_lower, "blk", down)
    pieces = early + late
    coded, _ = lax.optimization_barrier((adjacency, for_upper))
    degree = jnp.sum(jnp.bitwise_and(coded, 3), axis=(1, 2)).astype(jnp.float32)
    (mine,) = aggregate([words], (4,), pieces, 16, 8)
    return finish(mine, from_below, from_above, degree, features, w_self, w_neigh, bias)


def solution(mesh):
    in_specs = (
        P(("blk", "rep"), None),
        P(("blk", "rep"), None),
        P(("blk", "rep"), None, None, None),
        P(),
        P(),
        P(),
    )
    out_specs = P(("blk", "rep"), None)
    return jax.shard_map(shards, mesh=mesh, in_specs=in_specs, out_specs=out_specs, check_vma=False)
```
